32 devices in a mesh: row: 4 (over x, core), col: 4 (over z), depth: 2 (over y).
Axes of the slice: x: 2, y: 2, z: 4, core: 2. Of those that a mesh axis runs over, the one named last changes fastest.
Arguments:
- amplitudes: bfloat16 [2, 128, 3072], P(None, 'col', ('row', 'depth')), may hold values from -6 to 6
- integrals: bfloat16 [2, 3072, 3072], P(None, ('row', 'depth'), 'col'), may hold values from -0.15625 to 0.15625
- occ_count: int32 [2], replicated, may hold values from 65 to 128, as said below
- virtual_pair_count: int32 [2], replicated, may hold values from 3009 to 3072, as said below
Outputs:
- ladder: bfloat16 [4, 768, 2, 128], P(None, ('row', 'depth'), None, 'col')
The draws below stay inside these ranges and needn't reach their ends.
Inputs may be any that keep to these rules, and one draw needn't show every extreme that they name: `occ_count`: slots from the count up to 128 are padding; some block is full. `virtual_pair_count`: slots from the count up to 3072 are padding; some block is full.
All inputs are finite; a program needn't handle non-finite values.
Results may differ from the reference program's by a relative error of at most 0.001.
Values may be sent and summed in bfloat16 or wider, within the bound.
No kernel may reach another device: no remote copies, remote signals or barrier semaphores. Data moves between devices by JAX's collectives and lax.ppermute only.
A program may use at most 64 MiB of HBM per device.

```python
import jax
import jax.numpy as jnp
from jax import lax

IRREPS = 2
OB = 128
VB = 3072
NCB = 4
NB = 768


def live_count(key, capacity, leeway):
    offsets = jax.random.randint(key, (IRREPS,), 0, leeway + 1)
    full_block = jax.random.randint(jax.random.fold_in(key, 1), (), 0, IRREPS)
    slot_positions = jnp.arange(IRREPS, dtype=jnp.int32)
    offsets = jnp.where(slot_positions == full_block, 0, offsets)
    return (capacity - offsets).astype(jnp.int32)


def draw_occ_count(key, part):
    key = jax.random.fold_in(key, 3)
    return live_count(key, OB, min(63, OB // 2))


def draw_virtual_pair_count(key, part):
    key = jax.random.fold_in(key, 7)
    return live_count(key, VB, min(63, VB // 2))


def strengthened(drawn, own_key, source, target, blocks, factor):
    def block_of(dim):
        return (jnp.arange(drawn.shape[dim]) // (drawn.shape[dim] // blocks)).reshape((-1,) + (1,) * (drawn.ndim - 1 - dim))

    one_side = jax.random.permutation(own_key, blocks)[block_of(target)]
    far = (block_of(target) + blocks // 2) % blocks
    return jnp.where((block_of(source) == one_side) | (block_of(source) == far), factor * drawn, drawn)


def levels(rng, dims, pieces, low, largest):
    def one(dim, shards_of):
        draws = jax.random.uniform(jax.random.fold_in(jax.random.fold_in(rng, 6), dim), (shards_of,), jnp.float32, low / len(pieces), largest / len(pieces))
        return jnp.repeat(jnp.exp(draws), dims[dim] // shards_of).reshape((-1,) + (1,) * (len(dims) - dim - 1))

    factor_of = one(*pieces[0])
    for cut in pieces[1:]:
        factor_of = factor_of * one(*cut)
    return factor_of


def scatter_about(key, shape, spread, reach, cuts=(), held_as=jnp.bfloat16):
    factor_of = levels(key, shape, cuts, -0.22, 0.18) if cuts else 1.0
    values = jax.random.normal(key, shape, jnp.float32) * spread * factor_of
    return jnp.minimum(jnp.maximum(values, -reach), reach).astype(held_as)


def bell_draw_with(key, shape, width, reach, shards, heavy, kind=jnp.bfloat16):
    array = width * jax.random.normal(key, shape, jnp.float32)
    if shards:
        array = array * levels(key, shape, shards, -0.22, 0.18)
    return jnp.clip(strengthened(array, jax.random.fold_in(key, 3), *heavy), -reach, reach).astype(kind)


def setup_inputs(seed: int = 0) -> dict:
    arg_keys = jax.random.split(jax.random.key(seed), 5)
    return {
        "amplitudes": scatter_about(arg_keys[0], (IRREPS, OB, VB), 1.0, 6.0, ((1, 4), (2, 8))),
        "integrals": bell_draw_with(arg_keys[1], (IRREPS, VB, VB), VB ** -0.5, 0.15625, ((1, 8), (2, 4)), (1, 2, 8, 2.0)),
        "occ_count": draw_occ_count(jax.random.fold_in(arg_keys[4], 71), 0),
        "virtual_pair_count": draw_virtual_pair_count(jax.random.fold_in(arg_keys[4], 71), 0),
    }


def reference(amplitudes, integrals, occ_count, virtual_pair_count):
    vir_slots = jnp.arange(VB, dtype=jnp.int32)
    occupied_slot_range = jnp.arange(OB, dtype=jnp.int32)
    amp_live = (occupied_slot_range[None, :, None] < occ_count[:, None, None]) & (vir_slots[None, None, :] < virtual_pair_count[:, None, None])
    masked_amp = jnp.where(amp_live, amplitudes, jnp.zeros_like(amplitudes))

    def one_block(block):
        irrep = (block // NCB).astype(jnp.int32)
        column = (block % NCB).astype(jnp.int32)
        start = (column * NB).astype(jnp.int32)
        columns = lax.dynamic_slice(integrals, (irrep, jnp.int32(0), start), (1, VB, NB))[0]
        live = virtual_pair_count[irrep]
        rows_live = vir_slots < live
        cols_live = (start + jnp.arange(NB, dtype=jnp.int32)) < live
        masked_int = jnp.where(rows_live[:, None] & cols_live[None, :], columns, jnp.zeros_like(columns))
        amplitude_tile = lax.dynamic_index_in_dim(masked_amp, irrep, 0, keepdims=False)
        summed = lax.dot_general(masked_int, amplitude_tile, (((0,), (1,)), ((), ())), preferred_element_type=jnp.float32)
        return summed.astype(jnp.bfloat16)

    blocks = lax.map(one_block, jnp.arange(IRREPS * NCB, dtype=jnp.int32))
    return blocks.reshape(IRREPS, NCB, NB, OB).transpose(1, 2, 0, 3)
```

```python
import functools

import jax
import jax.numpy as jnp
from jax import lax
from jax.experimental import pallas as pl
from jax.experimental.pallas import tpu as pltpu
from jax.sharding import PartitionSpec as P

F32 = jnp.float32
BF16 = jnp.bfloat16
AXES = ("row", "col", "depth")


def given_to(i, step, n):
    return i ^ step if n & (n - 1) == 0 else (i + step) % n


def got_from(i, step, n):
    return i ^ step if n & (n - 1) == 0 else lax.rem(i - step + n, n)


def products(sizes, *refs):
    _, cols, depths = sizes
    occ, live = refs[:2]
    amps = refs[2 : 2 + cols]
    ints, send, keep = refs[2 + cols :]
    row, col, dep = (lax.axis_index(a) for a in AXES)
    core = lax.rem(row, 2)
    irreps, mb, kb = amps[0].shape
    kstart = (row * depths + dep) * kb
    wide = cols * mb
    nhalf = send.shape[1]
    for g in range(irreps):
        k_live = kstart + lax.broadcasted_iota(jnp.int32, (mb, kb), 1) < live[g]
        parts = []
        for j in range(cols):
            m = got_from(col, j, cols) * mb + lax.broadcasted_iota(jnp.int32, (mb, kb), 0)
            parts.append(jnp.where(k_live & (m < occ[g]), amps[j][g].astype(F32), 0.0))
        lhs = jnp.concatenate(parts, axis=0).astype(BF16)
        out = jnp.dot(lhs, ints[g], preferred_element_type=F32).T
        for x in range(sizes[0] // 2):
            at = slice(g * wide, (g + 1) * wide)
            first = out[2 * x * nhalf : (2 * x + 1) * nhalf]
            second = out[(2 * x + 1) * nhalf : (2 * x + 2) * nhalf]
            send[x, :, at] = jnp.where(core == 0, second, first)
            keep[x, :, at] = jnp.where(core == 0, first, second)


def pieces(sizes, steps, keep, came, *outs):
    rows, _, depths = sizes
    x = lax.axis_index("row") // 2
    dep = lax.axis_index("depth")
    h = outs[0].shape[0]
    for (sx, sd), out in zip(steps, outs):
        tx = given_to(x, sx, rows // 2)
        at = pl.ds(pl.multiple_of(given_to(dep, sd, depths) * h, 8), h)
        out[...] = keep[tx, at, :] + came[tx, at, :]


def finish(sizes, *refs):
    rows, cols, depths = sizes
    live = refs[0]
    outs = refs[-cols:]
    ins = refs[1:-cols]
    row, col, dep = (lax.axis_index(a) for a in AXES)
    h, lanes = ins[0].shape
    irreps = live.shape[0]
    wide = lanes // irreps
    mb = wide // cols
    total = ins[0][...]
    for ref in ins[1:]:
        total = total + ref[...]
    pad = -h % 128
    if pad:
        total = jnp.concatenate([total, jnp.zeros((pad, lanes), F32)], axis=0)
    slot = (col * rows * depths + row * depths + dep) * h + lax.broadcasted_iota(jnp.int32, (wide, h), 1)
    for g in range(irreps):
        turned = total[:, g * wide : (g + 1) * wide].T[:, :h]
        turned = jnp.where(slot < live[g], turned, 0.0)
        for j in range(cols):
            outs[j][g] = turned[j * mb : (j + 1) * mb].astype(BF16)


def assemble(cols, *refs):
    out = refs[-1]
    col = lax.axis_index("col")
    for j in range(cols):
        out[got_from(col, j, cols)] = refs[j][...]


VMEM = pl.BlockSpec(memory_space=pltpu.VMEM)
SMEM = pl.BlockSpec(memory_space=pltpu.SMEM)


def call(kernel, name, smem, outs, *args):
    many = isinstance(outs, list)
    return pl.pallas_call(
        kernel,
        name=name,
        out_shape=outs,
        in_specs=[SMEM] * smem + [VMEM] * (len(args) - smem),
        out_specs=[VMEM] * len(outs) if many else VMEM,
        compiler_params=pltpu.CompilerParams(vmem_limit_bytes=48 * 2**20),
    )(*args)


def body(sizes, amplitudes, integrals, occ_count, virtual_pair_count):
    rows, cols, depths = sizes
    chips = rows // 2
    irreps, mb, _ = amplitudes.shape
    nb = integrals.shape[2]
    h = nb // (rows * depths)
    lanes = irreps * cols * mb

    amps = [amplitudes]
    for j in range(1, cols):
        amps.append(lax.ppermute(amplitudes, "col", [(i, given_to(i, j, cols)) for i in range(cols)]))

    half = jax.ShapeDtypeStruct((chips, depths * h, lanes), F32)
    send, keep = call(
        functools.partial(products, sizes), "products", 2, [half, half],
        occ_count, virtual_pair_count, *amps, integrals,
    )
    came = lax.ppermute(send, "row", [(i, i ^ 1) for i in range(rows)])

    steps = [(sx, sd) for sx in range(chips) for sd in range(depths)]
    piece = jax.ShapeDtypeStruct((h, lanes), F32)
    out = call(functools.partial(pieces, sizes, steps), "pieces", 0, [piece] * len(steps), keep, came)
    sums = [out[0]]
    for (sx, sd), part in list(zip(steps, out))[1:]:
        pairs = []
        for row in range(rows):
            for dep in range(depths):
                to = (given_to(row // 2, sx, chips) * 2 + row % 2) * depths + given_to(dep, sd, depths)
                pairs.append((row * depths + dep, to))
        sums.append(lax.ppermute(part, ("row", "depth"), pairs))

    block = jax.ShapeDtypeStruct((irreps, mb, h), BF16)
    done = call(functools.partial(finish, sizes), "finish", 1, [block] * cols, virtual_pair_count, *sums)
    back = [done[0]]
    for j in range(1, cols):
        pairs = [(given_to(i, j, cols), i) for i in range(cols)]
        back.append(lax.ppermute(done[j], "col", pairs))
    whole = jax.ShapeDtypeStruct((cols, irreps, mb, h), BF16)
    result = call(functools.partial(assemble, cols), "assemble", 0, whole, *back)
    return result.transpose(0, 3, 1, 2)


def solution(mesh):
    sizes = tuple(mesh.shape[a] for a in AXES)
    in_specs = (P(None, "col", ("row", "depth")), P(None, ("row", "depth"), "col"), P(), P())
    out_specs = P(None, ("row", "depth"), None, "col")
    return jax.shard_map(
        functools.partial(body, sizes), mesh=mesh, in_specs=in_specs, out_specs=out_specs, check_vma=False
    )
```

```python
import functools

import jax
import jax.numpy as jnp
from jax import lax
from jax.experimental import pallas as pl
from jax.experimental.pallas import tpu as pltpu
from jax.sharding import PartitionSpec as P

F32 = jnp.float32
BF16 = jnp.bfloat16
AXES = ("row", "col", "depth")
VMEM = pl.BlockSpec(memory_space=pltpu.VMEM)
SMEM = pl.BlockSpec(memory_space=pltpu.SMEM)
HBM = pl.BlockSpec(memory_space=pl.ANY)


def load(occ, live, ints, held, limits, sem):
    copies = [pltpu.make_async_copy(ints.at[g], held.at[g], sem.at[g]) for g in range(ints.shape[0])]
    for copy in copies:
        copy.start()
    for g in range(ints.shape[0]):
        limits[0, g] = jnp.full(limits.shape[2:], occ[g], jnp.int32)
        limits[1, g] = jnp.full(limits.shape[2:], live[g], jnp.int32)
    for copy in copies:
        copy.wait()


def join(mine, other, both):
    both[0] = mine[...]
    both[1] = other[...]


def chunk_masks(cols):
    half = cols // 2
    return list(range(half)), list(range(half, cols))


def products(sizes, steps, *refs):
    rows, cols, depths = sizes
    half = cols // 2
    limits, mine = refs[:2]
    came = refs[2 : 2 + half]
    ints, ints_other = refs[2 + half : 4 + half]
    outs = refs[4 + half : -1]
    turned = refs[-1]
    row, col, dep = (lax.axis_index(a) for a in AXES)
    core = lax.rem(row, 2)
    _, irreps, mb, kb = mine.shape
    row_of = (row, row ^ 1)
    for g in range(irreps):
        total = None
        for part in range(2):
            kstart = (row_of[part] * depths + dep) * kb
            live = limits[1, g][:1, :1]
            k_live = kstart + lax.broadcasted_iota(jnp.int32, (mb, kb), 1) < live
            lhs = []
            for q in range(half):
                m = (col ^ (q + core * half)) * mb + lax.broadcasted_iota(jnp.int32, (mb, kb), 0)
                amp = came[q][part, g].astype(F32)
                if q == 0:
                    amp = jnp.where(core == 0, mine[part, g].astype(F32), amp)
                lhs.append(jnp.where(k_live & (m < limits[0, g][:1, :1]), amp, 0.0))
            lhs = jnp.concatenate(lhs, axis=0).astype(BF16)
            term = jnp.dot(lhs, (ints, ints_other)[part][g], preferred_element_type=F32)
            total = term if total is None else total + term
        wide = half * mb
        turned[:, g * wide : (g + 1) * wide] = total.T
    h = outs[0].shape[0] // 2
    for (sx, sd), out in zip(steps, outs):
        for c in range(2):
            block = ((row // 2 ^ sx) * 2 + c) * depths + (dep ^ sd)
            out[c * h : (c + 1) * h] = turned[pl.ds(pl.multiple_of(block * h, 8), h), :]


def finish(sizes, *refs):
    rows, cols, depths = sizes
    half = cols // 2
    limits = refs[0]
    outs = refs[-half:]
    ins = refs[1:-half]
    row, col, dep = (lax.axis_index(a) for a in AXES)
    core = lax.rem(row, 2)
    _, irreps, mb, h = outs[0].shape
    total = ins[0][...]
    for ref in ins[1:]:
        total = total + ref[...]
    lanes = total.shape[1]
    for c in range(2):
        part = total[c * h : (c + 1) * h]
        if h % 128:
            part = jnp.concatenate([part, jnp.zeros((-h % 128, lanes), F32)], axis=0)
        part = part.T[:, :h]
        slot = ((col * rows + row - core + c) * depths + dep) * h + lax.broadcasted_iota(jnp.int32, (mb, h), 1)
        for g in range(irreps):
            for q in range(half):
                at = (g * half + q) * mb
                outs[q][c, g] = jnp.where(slot < limits[1, g][:1, :1], part[at : at + mb], 0.0).astype(BF16)


def settle(half, *refs):
    first, came, keep, send = refs[0], refs[1 : 1 + half], refs[-2], refs[-1]
    core = lax.rem(lax.axis_index("row"), 2)
    for ref, c in ((keep, core), (send, 1 - core)):
        ref[0] = jnp.where(core == 0, first[c].astype(F32), came[0][c].astype(F32)).astype(BF16)
        for q in range(1, half):
            ref[q] = came[q][c]


def assemble(half, keep, came, out):
    core = lax.rem(lax.axis_index("row"), 2)
    col = lax.axis_index("col")
    for q in range(half):
        out[col ^ (q + core * half)] = keep[q]
        out[col ^ (q + (1 - core) * half)] = came[q]


def call(kernel, name, specs, outs, *args, scratch=(), cost=None):
    many = isinstance(outs, list)
    return pl.pallas_call(
        kernel,
        name=name,
        out_shape=outs,
        in_specs=specs + [VMEM] * (len(args) - len(specs)),
        out_specs=[VMEM] * len(outs) if many else VMEM,
        scratch_shapes=list(scratch),
        cost_estimate=cost,
        compiler_params=pltpu.CompilerParams(vmem_limit_bytes=40 * 2**20),
    )(*args)


def body(sizes, amplitudes, integrals, occ_count, virtual_pair_count):
    rows, cols, depths = sizes
    chips, half = rows // 2, cols // 2
    irreps, mb, kb = amplitudes.shape
    nb = integrals.shape[2]
    h = nb // (rows * depths)
    shape = jax.ShapeDtypeStruct

    def pairs(move):
        out = []
        for row in range(rows):
            for col in range(cols):
                for dep in range(depths):
                    r, c, d = move(row, col, dep)
                    out.append(((row * cols + col) * depths + dep, (r * cols + c) * depths + d))
        return out

    def send(value, move):
        return lax.ppermute(value, AXES, pairs(move))

    def other_core(row, col, dep):
        return row ^ 1, col, dep

    def chunk(q):
        def move(row, col, dep):
            if row % 2:
                return row, col ^ (q + half), dep
            return (row, col ^ q, dep) if q else (row ^ 2, col, dep)

        return move

    amps_other = send(amplitudes, other_core)
    ints_other = send(integrals, other_core)
    both = call(join, "join", [], shape((2, irreps, mb, kb), BF16), amplitudes, amps_other)
    came = [send(both, chunk(q)) for q in range(half)]
    ints, limits = call(
        load, "load", [SMEM, SMEM, HBM],
        [shape(integrals.shape, BF16), shape((2, irreps, 8, 128), jnp.int32)],
        occ_count, virtual_pair_count, integrals,
        scratch=[pltpu.SemaphoreType.DMA((irreps,))],
        cost=pl.CostEstimate(flops=0, bytes_accessed=4 * integrals.size, transcendentals=0),
    )

    steps = [(sx, sd) for sx in range(chips) for sd in range(depths)]
    lanes = irreps * half * mb
    out = call(
        functools.partial(products, sizes, steps), "products", [], [shape((2 * h, lanes), F32)] * len(steps),
        limits, both, *came, ints, ints_other,
        scratch=[pltpu.VMEM((nb, lanes), F32)],
    )
    sums = [out[0]]
    for (sx, sd), part in list(zip(steps, out))[1:]:
        sums.append(send(part, lambda row, col, dep, sx=sx, sd=sd: (row ^ 2 * sx, col, dep ^ sd)))

    done = call(
        functools.partial(finish, sizes), "finish", [], [shape((2, irreps, mb, h), BF16)] * half, limits, *sums
    )
    back = [send(done[q], chunk(q)) for q in range(half)]
    blocks = shape((half, irreps, mb, h), BF16)
    keep, give = call(functools.partial(settle, half), "settle", [], [blocks, blocks], done[0], *back)
    result = call(
        functools.partial(assemble, half), "assemble", [], shape((cols, irreps, mb, h), BF16),
        keep, send(give, other_core),
    )
    return result.transpose(0, 3, 1, 2)


def solution(mesh):
    sizes = tuple(mesh.shape[a] for a in AXES)
    in_specs = (P(None, "col", ("row", "depth")), P(None, ("row", "depth"), "col"), P(), P())
    out_specs = P(None, ("row", "depth"), None, "col")
    return jax.shard_map(
        functools.partial(body, sizes), mesh=mesh, in_specs=in_specs, out_specs=out_specs, check_vma=False
    )
```

```python
import functools

import jax
import jax.numpy as jnp
from jax import lax
from jax.experimental import pallas as pl
from jax.experimental.pallas import tpu as pltpu
from jax.sharding import PartitionSpec as P

F32 = jnp.float32
BF16 = jnp.bfloat16
AXES = ("row", "col", "depth")
VMEM = pl.BlockSpec(memory_space=pltpu.VMEM)
SMEM = pl.BlockSpec(memory_space=pltpu.SMEM)


def spread(occ, live, limits):
    for g in range(limits.shape[1]):
        limits[0, g] = jnp.full(limits.shape[2:], occ[g], jnp.int32)
        limits[1, g] = jnp.full(limits.shape[2:], live[g], jnp.int32)


def copy(src, dst):
    dst[...] = src[...]


def join(mine, other, both):
    both[0] = mine[...]
    both[1] = other[...]


def chunk_masks(cols):
    half = cols // 2
    return list(range(half)), list(range(half, cols))


def products(sizes, steps, *refs):
    rows, cols, depths = sizes
    half = cols // 2
    limits, mine = refs[:2]
    came = refs[2 : 2 + half]
    ints, ints_other = refs[2 + half : 4 + half]
    outs = refs[4 + half : -1]
    turned = refs[-1]
    row, col, dep = (lax.axis_index(a) for a in AXES)
    core = lax.rem(row, 2)
    _, irreps, mb, kb = mine.shape
    row_of = (row, row ^ 1)
    for g in range(irreps):
        total = None
        for part in range(2):
            kstart = (row_of[part] * depths + dep) * kb
            live = limits[1, g][:1, :1]
            k_live = kstart + lax.broadcasted_iota(jnp.int32, (mb, kb), 1) < live
            lhs = []
            for q in range(half):
                m = (col ^ (q + core * half)) * mb + lax.broadcasted_iota(jnp.int32, (mb, kb), 0)
                amp = came[q][part, g].astype(F32)
                if q == 0:
                    amp = jnp.where(core == 0, mine[part, g].astype(F32), amp)
                lhs.append(jnp.where(k_live & (m < limits[0, g][:1, :1]), amp, 0.0))
            lhs = jnp.concatenate(lhs, axis=0).astype(BF16)
            term = jnp.dot(lhs, (ints, ints_other)[part][g], preferred_element_type=F32)
            total = term if total is None else total + term
        wide = half * mb
        turned[:, g * wide : (g + 1) * wide] = total.T
    h = outs[0].shape[0] // 2
    for (sx, sd), out in zip(steps, outs):
        for c in range(2):
            block = ((row // 2 ^ sx) * 2 + c) * depths + (dep ^ sd)
            out[c * h : (c + 1) * h] = turned[pl.ds(pl.multiple_of(block * h, 8), h), :]


def finish(sizes, *refs):
    rows, cols, depths = sizes
    half = cols // 2
    limits = refs[0]
    outs = refs[-half:]
    ins = refs[1:-half]
    row, col, dep = (lax.axis_index(a) for a in AXES)
    core = lax.rem(row, 2)
    _, irreps, mb, h = outs[0].shape
    total = ins[0][...]
    for ref in ins[1:]:
        total = total + ref[...]
    lanes = total.shape[1]
    for c in range(2):
        part = total[c * h : (c + 1) * h]
        if h % 128:
            part = jnp.concatenate([part, jnp.zeros((-h % 128, lanes), F32)], axis=0)
        part = part.T[:, :h]
        slot = ((col * rows + row - core + c) * depths + dep) * h + lax.broadcasted_iota(jnp.int32, (mb, h), 1)
        for g in range(irreps):
            for q in range(half):
                at = (g * half + q) * mb
                outs[q][c, g] = jnp.where(slot < limits[1, g][:1, :1], part[at : at + mb], 0.0).astype(BF16)


def settle(half, *refs):
    first, came, keep, send = refs[0], refs[1 : 1 + half], refs[-2], refs[-1]
    core = lax.rem(lax.axis_index("row"), 2)
    for ref, c in ((keep, core), (send, 1 - core)):
        ref[0] = jnp.where(core == 0, first[c].astype(F32), came[0][c].astype(F32)).astype(BF16)
        for q in range(1, half):
            ref[q] = came[q][c]


def assemble(half, keep, came, out):
    core = lax.rem(lax.axis_index("row"), 2)
    col = lax.axis_index("col")
    for q in range(half):
        out[col ^ (q + core * half)] = keep[q]
        out[col ^ (q + (1 - core) * half)] = came[q]


def call(kernel, name, specs, outs, *args, scratch=()):
    many = isinstance(outs, list)
    return pl.pallas_call(
        kernel,
        name=name,
        out_shape=outs,
        in_specs=specs + [VMEM] * (len(args) - len(specs)),
        out_specs=[VMEM] * len(outs) if many else VMEM,
        scratch_shapes=list(scratch),
        compiler_params=pltpu.CompilerParams(vmem_limit_bytes=40 * 2**20),
    )(*args)


def body(sizes, amplitudes, integrals, occ_count, virtual_pair_count):
    rows, cols, depths = sizes
    chips, half = rows // 2, cols // 2
    irreps, mb, kb = amplitudes.shape
    nb = integrals.shape[2]
    h = nb // (rows * depths)
    shape = jax.ShapeDtypeStruct

    def pairs(move):
        out = []
        for row in range(rows):
            for col in range(cols):
                for dep in range(depths):
                    r, c, d = move(row, col, dep)
                    out.append(((row * cols + col) * depths + dep, (r * cols + c) * depths + d))
        return out

    def send(value, move):
        return lax.ppermute(value, AXES, pairs(move))

    def other_core(row, col, dep):
        return row ^ 1, col, dep

    def chunk(q):
        def move(row, col, dep):
            if row % 2:
                return row, col ^ (q + half), dep
            return (row, col ^ q, dep) if q else (row ^ 2, col, dep)

        return move

    amps_other = send(amplitudes, other_core)
    ints = call(copy, "load", [], shape(integrals.shape, BF16), integrals)
    limits = call(
        spread, "spread", [SMEM, SMEM], shape((2, irreps, 8, 128), jnp.int32), occ_count, virtual_pair_count
    )
    mine = call(copy, "fetch", [], shape(amplitudes.shape, BF16), amplitudes)
    both = call(join, "join", [], shape((2, irreps, mb, kb), BF16), mine, amps_other)
    later, both = lax.optimization_barrier((integrals, both))
    ints_other = send(later, other_core)
    came = [send(both, chunk(q)) for q in range(half)]

    steps = [(sx, sd) for sx in range(chips) for sd in range(depths)]
    lanes = irreps * half * mb
    out = call(
        functools.partial(products, sizes, steps), "products", [], [shape((2 * h, lanes), F32)] * len(steps),
        limits, both, *came, ints, ints_other,
        scratch=[pltpu.VMEM((nb, lanes), F32)],
    )
    sums = [out[0]]
    for (sx, sd), part in list(zip(steps, out))[1:]:
        sums.append(send(part, lambda row, col, dep, sx=sx, sd=sd: (row ^ 2 * sx, col, dep ^ sd)))

    done = call(
        functools.partial(finish, sizes), "finish", [], [shape((2, irreps, mb, h), BF16)] * half, limits, *sums
    )
    back = [send(done[q], chunk(q)) for q in range(half)]
    blocks = shape((half, irreps, mb, h), BF16)
    keep, give = call(functools.partial(settle, half), "settle", [], [blocks, blocks], done[0], *back)
    result = call(
        functools.partial(assemble, half), "assemble", [], shape((cols, irreps, mb, h), BF16),
        keep, send(give, other_core),
    )
    return result.transpose(0, 3, 1, 2)


def solution(mesh):
    sizes = tuple(mesh.shape[a] for a in AXES)
    in_specs = (P(None, "col", ("row", "depth")), P(None, ("row", "depth"), "col"), P(), P())
    out_specs = P(None, ("row", "depth"), None, "col")
    return jax.shard_map(
        functools.partial(body, sizes), mesh=mesh, in_specs=in_specs, out_specs=out_specs, check_vma=False
    )
```

```python
import functools

import jax
import jax.numpy as jnp
from jax import lax
from jax.experimental import pallas as pl
from jax.experimental.pallas import tpu as pltpu
from jax.sharding import PartitionSpec as P

F32 = jnp.float32
BF16 = jnp.bfloat16
AXES = ("row", "col", "depth")
VMEM = pl.BlockSpec(memory_space=pltpu.VMEM)
SMEM = pl.BlockSpec(memory_space=pltpu.SMEM)


def spread(occ, live, limits):
    for g in range(limits.shape[1]):
        limits[0, g] = jnp.full(limits.shape[2:], occ[g], jnp.int32)
        limits[1, g] = jnp.full(limits.shape[2:], live[g], jnp.int32)


def copy(src, dst):
    dst[...] = src[...]


def join(mine, other, both):
    both[0] = mine[...]
    both[1] = other[...]


def products(sizes, steps, *refs):
    rows, cols, depths = sizes
    half = cols // 2
    limits, mine = refs[:2]
    came = refs[2 : 2 + half]
    ints, ints_other = refs[2 + half : 4 + half]
    outs = refs[4 + half : -1]
    turned = refs[-1]
    row, col, dep = (lax.axis_index(a) for a in AXES)
    core = lax.rem(row, 2)
    _, irreps, mb, kb = mine.shape
    row_of = (row, row ^ 1)
    for g in range(irreps):
        total = None
        for part in range(2):
            kstart = (row_of[part] * depths + dep) * kb
            live = limits[1, g][:1, :1]
            k_live = kstart + lax.broadcasted_iota(jnp.int32, (mb, kb), 1) < live
            lhs = []
            for q in range(half):
                m = (col ^ (q + core * half)) * mb + lax.broadcasted_iota(jnp.int32, (mb, kb), 0)
                amp = came[q][part, g].astype(F32)
                if q == 0:
                    amp = jnp.where(core == 0, mine[part, g].astype(F32), amp)
                lhs.append(jnp.where(k_live & (m < limits[0, g][:1, :1]), amp, 0.0))
            lhs = jnp.concatenate(lhs, axis=0).astype(BF16)
            term = jnp.dot(lhs, (ints, ints_other)[part][g], preferred_element_type=F32)
            total = term if total is None else total + term
        wide = half * mb
        turned[:, g * wide : (g + 1) * wide] = total.T
    h = outs[0].shape[0] // 2
    for (sx, sd), out in zip(steps, outs):
        for c in range(2):
            block = ((row // 2 ^ sx) * 2 + c) * depths + (dep ^ sd)
            out[c * h : (c + 1) * h] = turned[pl.ds(pl.multiple_of(block * h, 8), h), :]


def finish(sizes, *refs):
    rows, cols, depths = sizes
    half = cols // 2
    limits = refs[0]
    outs = refs[-half:]
    ins = refs[1:-half]
    row, col, dep = (lax.axis_index(a) for a in AXES)
    core = lax.rem(row, 2)
    _, irreps, mb, h = outs[0].shape
    total = ins[0][...]
    for ref in ins[1:]:
        total = total + ref[...]
    lanes = total.shape[1]
    for c in range(2):
        part = total[c * h : (c + 1) * h]
        if h % 128:
            part = jnp.concatenate([part, jnp.zeros((-h % 128, lanes), F32)], axis=0)
        part = part.T[:, :h]
        slot = ((col * rows + row - core + c) * depths + dep) * h + lax.broadcasted_iota(jnp.int32, (mb, h), 1)
        for g in range(irreps):
            for q in range(half):
                at = (g * half + q) * mb
                outs[q][c, g] = jnp.where(slot < limits[1, g][:1, :1], part[at : at + mb], 0.0).astype(BF16)


def settle(half, *refs):
    back, give = refs[:half][::-1], refs[-1]
    core = lax.rem(lax.axis_index("row"), 2)
    for q in range(half):
        give[q] = back[q][1 - core]


def assemble(half, first, *refs):
    back, came, out = refs[:half][::-1], refs[-2], refs[-1]
    core = lax.rem(lax.axis_index("row"), 2)
    col = lax.axis_index("col")

    def pick(zero, one):
        return jnp.where(core == 0, zero.astype(F32), one.astype(F32)).astype(BF16)

    out[col] = pick(first[0], back[0][1])
    out[col ^ half] = pick(back[0][0], came[0])
    for q in range(1, half):
        out[col ^ (q + core * half)] = back[q][core]
        out[col ^ (q + (1 - core) * half)] = came[q]


def call(kernel, name, specs, outs, *args, scratch=()):
    many = isinstance(outs, list)
    return pl.pallas_call(
        kernel,
        name=name,
        out_shape=outs,
        in_specs=specs + [VMEM] * (len(args) - len(specs)),
        out_specs=[VMEM] * len(outs) if many else VMEM,
        scratch_shapes=list(scratch),
        compiler_params=pltpu.CompilerParams(vmem_limit_bytes=40 * 2**20),
    )(*args)


def body(sizes, amplitudes, integrals, occ_count, virtual_pair_count):
    rows, cols, depths = sizes
    chips, half = rows // 2, cols // 2
    irreps, mb, kb = amplitudes.shape
    nb = integrals.shape[2]
    h = nb // (rows * depths)
    shape = jax.ShapeDtypeStruct

    def pairs(move):
        out = []
        for row in range(rows):
            for col in range(cols):
                for dep in range(depths):
                    r, c, d = move(row, col, dep)
                    out.append(((row * cols + col) * depths + dep, (r * cols + c) * depths + d))
        return out

    def send(value, move):
        return lax.ppermute(value, AXES, pairs(move))

    def other_core(row, col, dep):
        return row ^ 1, col, dep

    def chunk(q):
        def move(row, col, dep):
            if row % 2:
                return row, col ^ (q + half), dep
            return (row, col ^ q, dep) if q else (row ^ 2, col, dep)

        return move

    amps_other = send(amplitudes, other_core)
    ints = call(copy, "load", [], shape(integrals.shape, BF16), integrals)
    limits = call(
        spread, "spread", [SMEM, SMEM], shape((2, irreps, 8, 128), jnp.int32), occ_count, virtual_pair_count
    )
    mine = call(copy, "fetch", [], shape(amplitudes.shape, BF16), amplitudes)
    both = call(join, "join", [], shape((2, irreps, mb, kb), BF16), mine, amps_other)
    later, both = lax.optimization_barrier((integrals, both))
    ints_other = send(later, other_core)
    came = [send(both, chunk(q)) for q in range(half)]

    steps = [(sx, sd) for sx in range(chips) for sd in reversed(range(depths))]
    steps = [(0, 0)] + [step for step in steps if any(step)]
    lanes = irreps * half * mb
    out = call(
        functools.partial(products, sizes, steps), "products", [], [shape((2 * h, lanes), F32)] * len(steps),
        limits, both, *came, ints, ints_other,
        scratch=[pltpu.VMEM((nb, lanes), F32)],
    )
    sums = [out[0]]
    for (sx, sd), part in zip(steps[1:], out[1:]):
        sums.append(send(part, lambda row, col, dep, sx=sx, sd=sd: (row ^ 2 * sx, col, dep ^ sd)))

    done = call(
        functools.partial(finish, sizes), "finish", [], [shape((2, irreps, mb, h), BF16)] * half, limits, *sums
    )
    def home(row, col, dep):
        return (row ^ 1, col ^ half, dep) if row % 2 else (row ^ 1, col, dep)

    back = [send(done[q], chunk(q) if q else home) for q in range(half)]
    give = call(functools.partial(settle, half), "settle", [], shape((half, irreps, mb, h), BF16), *back[::-1])
    result = call(
        functools.partial(assemble, half), "assemble", [], shape((cols, irreps, mb, h), BF16),
        done[0], *back[::-1], send(give, other_core),
    )
    return result.transpose(0, 3, 1, 2)


def solution(mesh):
    sizes = tuple(mesh.shape[a] for a in AXES)
    in_specs = (P(None, "col", ("row", "depth")), P(None, ("row", "depth"), "col"), P(), P())
    out_specs = P(None, ("row", "depth"), None, "col")
    return jax.shard_map(
        functools.partial(body, sizes), mesh=mesh, in_specs=in_specs, out_specs=out_specs, check_vma=False
    )
```

```python
import functools

import jax
import jax.numpy as jnp
from jax import lax
from jax.experimental import pallas as pl
from jax.experimental.pallas import tpu as pltpu
from jax.sharding import PartitionSpec as P

F32 = jnp.float32
BF16 = jnp.bfloat16
AXES = ("row", "col", "depth")
VMEM = pl.BlockSpec(memory_space=pltpu.VMEM)
SMEM = pl.BlockSpec(memory_space=pltpu.SMEM)


def spread(occ, live, limits):
    for g in range(limits.shape[1]):
        limits[0, g] = jnp.full(limits.shape[2:], occ[g], jnp.int32)
        limits[1, g] = jnp.full(limits.shape[2:], live[g], jnp.int32)


def copy(src, dst):
    dst[...] = src[...]


def join(mine, other, both):
    both[0] = mine[...]
    both[1] = other[...]


def products(sizes, steps, *refs):
    rows, cols, depths = sizes
    half = cols // 2
    limits, mine = refs[:2]
    came = refs[2 : 2 + half]
    ints, ints_other = refs[2 + half : 4 + half]
    outs = refs[4 + half : -1]
    turned = refs[-1]
    row, col, dep = (lax.axis_index(a) for a in AXES)
    core = lax.rem(row, 2)
    _, irreps, mb, kb = mine.shape
    row_of = (row, row ^ 1)
    totals = []
    for g in range(irreps):
        total = None
        for part in range(2):
            kstart = (row_of[part] * depths + dep) * kb
            live = limits[1, g][:1, :1]
            k_live = kstart + lax.broadcasted_iota(jnp.int32, (mb, kb), 1) < live
            lhs = []
            for q in range(half):
                m = (col ^ (q + core * half)) * mb + lax.broadcasted_iota(jnp.int32, (mb, kb), 0)
                amp = came[q][part, g].astype(F32)
                if q == 0:
                    amp = jnp.where(core == 0, mine[part, g].astype(F32), amp)
                lhs.append(jnp.where(k_live & (m < limits[0, g][:1, :1]), amp, 0.0))
            lhs = jnp.concatenate(lhs, axis=0).astype(BF16)
            term = jnp.dot(lhs, (ints, ints_other)[part][g], preferred_element_type=F32)
            total = term if total is None else total + term
        totals.append(total)
    turned[...] = jnp.concatenate(totals, axis=0).T
    h = outs[0].shape[0] // 2
    for (sx, sd), out in zip(steps, outs):
        for c in range(2):
            block = ((row // 2 ^ sx) * 2 + c) * depths + (dep ^ sd)
            out[c * h : (c + 1) * h] = turned[pl.ds(pl.multiple_of(block * h, 8), h), :]


def finish(sizes, *refs):
    rows, cols, depths = sizes
    half = cols // 2
    limits = refs[0]
    outs = refs[-half:]
    ins = refs[1:-half]
    row, col, dep = (lax.axis_index(a) for a in AXES)
    core = lax.rem(row, 2)
    _, irreps, mb, h = outs[0].shape
    total = ins[0][...]
    for ref in ins[1:]:
        total = total + ref[...]
    lanes = total.shape[1]
    for c in range(2):
        part = total[c * h : (c + 1) * h]
        if h % 128:
            part = jnp.concatenate([part, jnp.zeros((-h % 128, lanes), F32)], axis=0)
        part = part.T[:, :h]
        slot = ((col * rows + row - core + c) * depths + dep) * h + lax.broadcasted_iota(jnp.int32, (mb, h), 1)
        for g in range(irreps):
            for q in range(half):
                at = (g * half + q) * mb
                outs[q][c, g] = jnp.where(slot < limits[1, g][:1, :1], part[at : at + mb], 0.0).astype(BF16)


def settle(half, *refs):
    back, give = refs[:half][::-1], refs[-1]
    core = lax.rem(lax.axis_index("row"), 2)
    for q in range(half):
        give[q] = back[q][1 - core]


def assemble(half, first, *refs):
    back, came, out = refs[:half][::-1], refs[-2], refs[-1]
    core = lax.rem(lax.axis_index("row"), 2)
    col = lax.axis_index("col")

    def pick(zero, one):
        return jnp.where(core == 0, zero.astype(F32), one.astype(F32)).astype(BF16)

    out[col] = pick(first[0], back[0][1])
    out[col ^ half] = pick(back[0][0], came[0])
    for q in range(1, half):
        out[col ^ (q + core * half)] = back[q][core]
        out[col ^ (q + (1 - core) * half)] = came[q]


def call(kernel, name, specs, outs, *args, scratch=()):
    many = isinstance(outs, list)
    return pl.pallas_call(
        kernel,
        name=name,
        out_shape=outs,
        in_specs=specs + [VMEM] * (len(args) - len(specs)),
        out_specs=[VMEM] * len(outs) if many else VMEM,
        scratch_shapes=list(scratch),
        compiler_params=pltpu.CompilerParams(vmem_limit_bytes=40 * 2**20),
    )(*args)


def body(sizes, amplitudes, integrals, occ_count, virtual_pair_count):
    rows, cols, depths = sizes
    chips, half = rows // 2, cols // 2
    irreps, mb, kb = amplitudes.shape
    nb = integrals.shape[2]
    h = nb // (rows * depths)
    shape = jax.ShapeDtypeStruct

    def pairs(move):
        out = []
        for row in range(rows):
            for col in range(cols):
                for dep in range(depths):
                    r, c, d = move(row, col, dep)
                    out.append(((row * cols + col) * depths + dep, (r * cols + c) * depths + d))
        return out

    def send(value, move):
        return lax.ppermute(value, AXES, pairs(move))

    def other_core(row, col, dep):
        return row ^ 1, col, dep

    def chunk(q):
        def move(row, col, dep):
            if row % 2:
                return row, col ^ (q + half), dep
            return (row, col ^ q, dep) if q else (row ^ 2, col, dep)

        return move

    amps_other = send(amplitudes, other_core)
    ints = call(copy, "load", [], shape(integrals.shape, BF16), integrals)
    limits = call(
        spread, "spread", [SMEM, SMEM], shape((2, irreps, 8, 128), jnp.int32), occ_count, virtual_pair_count
    )
    mine = call(copy, "fetch", [], shape(amplitudes.shape, BF16), amplitudes)
    both = call(join, "join", [], shape((2, irreps, mb, kb), BF16), mine, amps_other)
    later, both = lax.optimization_barrier((integrals, both))
    ints_other = send(later, other_core)
    came = [send(both, chunk(q)) for q in range(half)]

    steps = [(sx, sd) for sx in range(chips) for sd in range(depths)]
    steps = steps[:1] + steps[:0:-1]
    lanes = irreps * half * mb
    out = call(
        functools.partial(products, sizes, steps), "products", [], [shape((2 * h, lanes), F32)] * len(steps),
        limits, both, *came, ints, ints_other,
        scratch=[pltpu.VMEM((nb, lanes), F32)],
    )
    sums = [out[0]]
    for (sx, sd), part in zip(steps[1:], out[1:]):
        sums.append(send(part, lambda row, col, dep, sx=sx, sd=sd: (row ^ 2 * sx, col, dep ^ sd)))

    done = call(
        functools.partial(finish, sizes), "finish", [], [shape((2, irreps, mb, h), BF16)] * half, limits, *sums
    )
    def home(row, col, dep):
        return (row ^ 1, col ^ half, dep) if row % 2 else (row ^ 1, col, dep)

    back = [send(done[q], chunk(q) if q else home) for q in range(half)]
    give = call(functools.partial(settle, half), "settle", [], shape((half, irreps, mb, h), BF16), *back[::-1])
    result = call(
        functools.partial(assemble, half), "assemble", [], shape((cols, irreps, mb, h), BF16),
        done[0], *back[::-1], send(give, other_core),
    )
    return result.transpose(0, 3, 1, 2)


def solution(mesh):
    sizes = tuple(mesh.shape[a] for a in AXES)
    in_specs = (P(None, "col", ("row", "depth")), P(None, ("row", "depth"), "col"), P(), P())
    out_specs = P(None, ("row", "depth"), None, "col")
    return jax.shard_map(
        functools.partial(body, sizes), mesh=mesh, in_specs=in_specs, out_specs=out_specs, check_vma=False
    )
```

```python
import functools

import jax
import jax.numpy as jnp
from jax import lax
from jax.experimental import pallas as pl
from jax.experimental.pallas import tpu as pltpu
from jax.sharding import PartitionSpec as P

F32 = jnp.float32
BF16 = jnp.bfloat16
AXES = ("row", "col", "depth")
VMEM = pl.BlockSpec(memory_space=pltpu.VMEM)
HBM = pl.BlockSpec(memory_space=pltpu.HBM)


def load(occ, live, ints, held, limits, counts, sem):
    irreps = ints.shape[0]
    copies = [(occ, counts.at[0]), (live, counts.at[1])] + [(ints.at[g], held.at[g]) for g in range(irreps)]
    copies = [pltpu.make_async_copy(src, dst, sem.at[i]) for i, (src, dst) in enumerate(copies)]
    for one in reversed(copies):
        one.start()
    for one in copies:
        one.wait()
    for kind in range(2):
        for g in range(irreps):
            limits[kind, g] = jnp.full(limits.shape[2:], counts[kind, g], jnp.int32)


def copy(src, dst):
    dst[...] = src[...]


def join(mine, other, both):
    both[0] = mine[...]
    both[1] = other[...]


def products(sizes, steps, *refs):
    rows, cols, depths = sizes
    half = cols // 2
    limits, mine = refs[:2]
    came = refs[2 : 2 + half]
    ints, ints_other = refs[2 + half : 4 + half]
    outs = refs[4 + half : -1]
    turned = refs[-1]
    row, col, dep = (lax.axis_index(a) for a in AXES)
    core = lax.rem(row, 2)
    _, irreps, mb, kb = mine.shape
    row_of = (row, row ^ 1)
    totals = []
    for g in range(irreps):
        total = None
        for part in range(2):
            kstart = (row_of[part] * depths + dep) * kb
            live = limits[1, g][:1, :1]
            k_live = kstart + lax.broadcasted_iota(jnp.int32, (mb, kb), 1) < live
            lhs = []
            for q in range(half):
                m = (col ^ (q + core * half)) * mb + lax.broadcasted_iota(jnp.int32, (mb, kb), 0)
                amp = came[q][part, g].astype(F32)
                if q == 0:
                    amp = jnp.where(core == 0, mine[part, g].astype(F32), amp)
                lhs.append(jnp.where(k_live & (m < limits[0, g][:1, :1]), amp, 0.0))
            lhs = jnp.concatenate(lhs, axis=0).astype(BF16)
            term = jnp.dot(lhs, (ints, ints_other)[part][g], preferred_element_type=F32)
            total = term if total is None else total + term
        totals.append(total)
    turned[...] = jnp.concatenate(totals, axis=0).T
    h = outs[0].shape[0] // 2
    for (sx, sd), out in zip(steps, outs):
        for c in range(2):
            block = ((row // 2 ^ sx) * 2 + c) * depths + (dep ^ sd)
            out[c * h : (c + 1) * h] = turned[pl.ds(pl.multiple_of(block * h, 8), h), :]


def finish(sizes, *refs):
    rows, cols, depths = sizes
    half = cols // 2
    limits = refs[0]
    outs = refs[-half:]
    ins = refs[1:-half]
    row, col, dep = (lax.axis_index(a) for a in AXES)
    core = lax.rem(row, 2)
    _, irreps, mb, h = outs[0].shape
    total = ins[0][...]
    for ref in ins[1:]:
        total = total + ref[...]
    lanes = total.shape[1]
    for c in range(2):
        part = total[c * h : (c + 1) * h]
        if h % 128:
            part = jnp.concatenate([part, jnp.zeros((-h % 128, lanes), F32)], axis=0)
        part = part.T[:, :h]
        slot = ((col * rows + row - core + c) * depths + dep) * h + lax.broadcasted_iota(jnp.int32, (mb, h), 1)
        for g in range(irreps):
            for q in range(half):
                at = (g * half + q) * mb
                outs[q][c, g] = jnp.where(slot < limits[1, g][:1, :1], part[at : at + mb], 0.0).astype(BF16)


def settle(half, *refs):
    back, give = refs[:half][::-1], refs[-1]
    core = lax.rem(lax.axis_index("row"), 2)
    for q in range(half):
        give[q] = back[q][1 - core]


def assemble(half, first, *refs):
    back, came, out = refs[:half][::-1], refs[-2], refs[-1]
    core = lax.rem(lax.axis_index("row"), 2)
    col = lax.axis_index("col")

    def pick(zero, one):
        return jnp.where(core == 0, zero.astype(F32), one.astype(F32)).astype(BF16)

    out[col] = pick(first[0], back[0][1])
    out[col ^ half] = pick(back[0][0], came[0])
    for q in range(1, half):
        out[col ^ (q + core * half)] = back[q][core]
        out[col ^ (q + (1 - core) * half)] = came[q]


def call(kernel, name, specs, outs, *args, scratch=()):
    many = isinstance(outs, list)
    return pl.pallas_call(
        kernel,
        name=name,
        out_shape=outs,
        in_specs=specs + [VMEM] * (len(args) - len(specs)),
        out_specs=[VMEM] * len(outs) if many else VMEM,
        scratch_shapes=list(scratch),
        compiler_params=pltpu.CompilerParams(vmem_limit_bytes=40 * 2**20),
    )(*args)


def body(sizes, amplitudes, integrals, occ_count, virtual_pair_count):
    rows, cols, depths = sizes
    chips, half = rows // 2, cols // 2
    irreps, mb, kb = amplitudes.shape
    nb = integrals.shape[2]
    h = nb // (rows * depths)
    shape = jax.ShapeDtypeStruct

    def pairs(move):
        out = []
        for row in range(rows):
            for col in range(cols):
                for dep in range(depths):
                    r, c, d = move(row, col, dep)
                    out.append(((row * cols + col) * depths + dep, (r * cols + c) * depths + d))
        return out

    def send(value, move):
        return lax.ppermute(value, AXES, pairs(move))

    def other_core(row, col, dep):
        return row ^ 1, col, dep

    def chunk(q):
        def move(row, col, dep):
            if row % 2:
                return row, col ^ (q + half), dep
            return (row, col ^ q, dep) if q else (row ^ 2, col, dep)

        return move

    amps_other = send(amplitudes, other_core)
    held = (occ_count, virtual_pair_count, integrals)
    held = [pltpu.with_memory_space_constraint(x, pltpu.HBM) for x in held]
    ints, limits = call(
        load, "load", [HBM] * 3, [shape(integrals.shape, BF16), shape((2, irreps, 8, 128), jnp.int32)], *held,
        scratch=[pltpu.SMEM((2, irreps), jnp.int32), pltpu.SemaphoreType.DMA((2 + irreps,))],
    )
    mine = call(copy, "fetch", [], shape(amplitudes.shape, BF16), amplitudes)
    both = call(join, "join", [], shape((2, irreps, mb, kb), BF16), mine, amps_other)
    later, both = lax.optimization_barrier((integrals, both))
    ints_other = send(later, other_core)
    came = [send(both, chunk(q)) for q in range(half)]

    steps = [(sx, sd) for sx in range(chips) for sd in range(depths)]
    steps = steps[:1] + steps[:0:-1]
    lanes = irreps * half * mb
    out = call(
        functools.partial(products, sizes, steps), "products", [], [shape((2 * h, lanes), F32)] * len(steps),
        limits, both, *came, ints, ints_other,
        scratch=[pltpu.VMEM((nb, lanes), F32)],
    )
    sums = [out[0]]
    for (sx, sd), part in zip(steps[1:], out[1:]):
        sums.append(send(part, lambda row, col, dep, sx=sx, sd=sd: (row ^ 2 * sx, col, dep ^ sd)))

    done = call(
        functools.partial(finish, sizes), "finish", [], [shape((2, irreps, mb, h), BF16)] * half, limits, *sums
    )
    def home(row, col, dep):
        return (row ^ 1, col ^ half, dep) if row % 2 else (row ^ 1, col, dep)

    back = [send(done[q], chunk(q) if q else home) for q in range(half)]
    give = call(functools.partial(settle, half), "settle", [], shape((half, irreps, mb, h), BF16), *back[::-1])
    result = call(
        functools.partial(assemble, half), "assemble", [], shape((cols, irreps, mb, h), BF16),
        done[0], *back[::-1], send(give, other_core),
    )
    return result.transpose(0, 3, 1, 2)


def solution(mesh):
    sizes = tuple(mesh.shape[a] for a in AXES)
    in_specs = (P(None, "col", ("row", "depth")), P(None, ("row", "depth"), "col"), P(), P())
    out_specs = P(None, ("row", "depth"), None, "col")
    return jax.shard_map(
        functools.partial(body, sizes), mesh=mesh, in_specs=in_specs, out_specs=out_specs, check_vma=False
    )
```

```python
import functools

import jax
import jax.numpy as jnp
from jax import lax
from jax.experimental import pallas as pl
from jax.experimental.pallas import tpu as pltpu
from jax.sharding import PartitionSpec as P

F32 = jnp.float32
BF16 = jnp.bfloat16
AXES = ("row", "col", "depth")
VMEM = pl.BlockSpec(memory_space=pltpu.VMEM)
HBM = pl.BlockSpec(memory_space=pltpu.HBM)


def load(occ, live, ints, held, limits, counts, sem):
    irreps = ints.shape[0]
    copies = [(occ, counts.at[0]), (live, counts.at[1])] + [(ints.at[g], held.at[g]) for g in range(irreps)]
    copies = [pltpu.make_async_copy(src, dst, sem.at[i]) for i, (src, dst) in enumerate(copies)]
    for one in reversed(copies):
        one.start()
    for one in copies:
        one.wait()
    for kind in range(2):
        for g in range(irreps):
            limits[kind, g] = jnp.full(limits.shape[2:], counts[kind, g], jnp.int32)


def copy(src, dst):
    dst[...] = src[...]


def join(mine, other, both):
    both[0] = mine[...]
    both[1] = other[...]


def products(sizes, steps, *refs):
    rows, cols, depths = sizes
    half = cols // 2
    limits, mine = refs[:2]
    came = refs[2 : 2 + half]
    ints, ints_other = refs[2 + half : 4 + half]
    outs = refs[4 + half : -1]
    turned = refs[-1]
    row, col, dep = (lax.axis_index(a) for a in AXES)
    core = lax.rem(row, 2)
    _, irreps, mb, kb = mine.shape
    row_of = (row, row ^ 1)
    totals = []
    for g in range(irreps):
        total = None
        for part in range(2):
            kstart = (row_of[part] * depths + dep) * kb
            live = limits[1, g][:1, :1]
            k_live = kstart + lax.broadcasted_iota(jnp.int32, (mb, kb), 1) < live
            lhs = []
            for q in range(half):
                m = (col ^ (q + core * half)) * mb + lax.broadcasted_iota(jnp.int32, (mb, kb), 0)
                amp = came[q][part, g].astype(F32)
                if q == 0:
                    amp = jnp.where(core == 0, mine[part, g].astype(F32), amp)
                lhs.append(jnp.where(k_live & (m < limits[0, g][:1, :1]), amp, 0.0))
            lhs = jnp.concatenate(lhs, axis=0).astype(BF16)
            term = jnp.dot(lhs, (ints, ints_other)[part][g], preferred_element_type=F32)
            total = term if total is None else total + term
        totals.append(total)
    turned[...] = jnp.concatenate(totals, axis=0).T
    h = outs[0].shape[0] // 2
    for (sx, sd), out in zip(steps, outs):
        for c in range(2):
            block = ((row // 2 ^ sx) * 2 + c) * depths + (dep ^ sd)
            out[c * h : (c + 1) * h] = turned[pl.ds(pl.multiple_of(block * h, 8), h), :]


def finish(sizes, *refs):
    rows, cols, depths = sizes
    half = cols // 2
    limits = refs[0]
    outs = refs[-half:]
    ins = refs[1:-half]
    row, col, dep = (lax.axis_index(a) for a in AXES)
    core = lax.rem(row, 2)
    _, irreps, mb, h = outs[0].shape
    total = ins[0][...]
    for ref in ins[1:]:
        total = total + ref[...]
    lanes = total.shape[1]
    for c in range(2):
        part = total[c * h : (c + 1) * h]
        if h % 128:
            part = jnp.concatenate([part, jnp.zeros((-h % 128, lanes), F32)], axis=0)
        part = part.T[:, :h]
        slot = ((col * rows + row - core + c) * depths + dep) * h + lax.broadcasted_iota(jnp.int32, (mb, h), 1)
        for g in range(irreps):
            for q in range(half):
                at = (g * half + q) * mb
                outs[q][c, g] = jnp.where(slot < limits[1, g][:1, :1], part[at : at + mb], 0.0).astype(BF16)


def settle(half, *refs):
    back, give = refs[:half][::-1], refs[-1]
    core = lax.rem(lax.axis_index("row"), 2)
    for q in range(half):
        give[q] = back[q][1 - core]


def pick(core, zero, one):
    return jnp.where(core == 0, zero.astype(F32), one.astype(F32)).astype(BF16)


def copy_all(sem, pairs):
    copies = [pltpu.make_async_copy(src, dst, sem.at[i]) for i, (src, dst) in enumerate(pairs)]
    for one in copies:
        one.start()
    for one in copies:
        one.wait()


def place(half, first, *refs):
    back, out, picked, sem = refs[:half][::-1], refs[-3], refs[-2], refs[-1]
    core = lax.rem(lax.axis_index("row"), 2)
    col = lax.axis_index("col")
    picked[...] = pick(core, first[0], back[0][1])
    pairs = [(back[q].at[core], out.at[col ^ (q + core * half)]) for q in range(1, half)]
    copy_all(sem, pairs + [(picked, out.at[col])])


def complete(half, far, came, placed, out, picked, sem):
    core = lax.rem(lax.axis_index("row"), 2)
    col = lax.axis_index("col")
    picked[...] = pick(core, far[0], came[0])
    pairs = [(came.at[q], out.at[col ^ (q + (1 - core) * half)]) for q in range(1, half)]
    copy_all(sem, pairs + [(picked, out.at[col ^ half])])


def call(kernel, name, specs, outs, *args, scratch=(), to=VMEM, last=(), aliases=None):
    many = isinstance(outs, list)
    return pl.pallas_call(
        kernel,
        name=name,
        out_shape=outs,
        in_specs=specs + [VMEM] * (len(args) - len(specs) - len(last)) + list(last),
        out_specs=[to] * len(outs) if many else to,
        input_output_aliases=aliases or {},
        scratch_shapes=list(scratch),
        compiler_params=pltpu.CompilerParams(vmem_limit_bytes=40 * 2**20),
    )(*args)


def body(sizes, amplitudes, integrals, occ_count, virtual_pair_count):
    rows, cols, depths = sizes
    chips, half = rows // 2, cols // 2
    irreps, mb, kb = amplitudes.shape
    nb = integrals.shape[2]
    h = nb // (rows * depths)
    shape = jax.ShapeDtypeStruct

    def pairs(move):
        out = []
        for row in range(rows):
            for col in range(cols):
                for dep in range(depths):
                    r, c, d = move(row, col, dep)
                    out.append(((row * cols + col) * depths + dep, (r * cols + c) * depths + d))
        return out

    def send(value, move):
        return lax.ppermute(value, AXES, pairs(move))

    def other_core(row, col, dep):
        return row ^ 1, col, dep

    def chunk(q):
        def move(row, col, dep):
            if row % 2:
                return row, col ^ (q + half), dep
            return (row, col ^ q, dep) if q else (row ^ 2, col, dep)

        return move

    amps_other = send(amplitudes, other_core)
    held = (occ_count, virtual_pair_count, integrals)
    held = [pltpu.with_memory_space_constraint(x, pltpu.HBM) for x in held]
    ints, limits = call(
        load, "load", [HBM] * 3, [shape(integrals.shape, BF16), shape((2, irreps, 8, 128), jnp.int32)], *held,
        scratch=[pltpu.SMEM((2, irreps), jnp.int32), pltpu.SemaphoreType.DMA((2 + irreps,))],
    )
    mine = call(copy, "fetch", [], shape(amplitudes.shape, BF16), amplitudes)
    both = call(join, "join", [], shape((2, irreps, mb, kb), BF16), mine, amps_other)
    later, both = lax.optimization_barrier((integrals, both))
    ints_other = send(later, other_core)
    came = [send(both, chunk(q)) for q in range(half)]

    steps = [(sx, sd) for sx in range(chips) for sd in range(depths)]
    steps = steps[:1] + steps[:0:-1]
    lanes = irreps * half * mb
    out = call(
        functools.partial(products, sizes, steps), "products", [], [shape((2 * h, lanes), F32)] * len(steps),
        limits, both, *came, ints, ints_other,
        scratch=[pltpu.VMEM((nb, lanes), F32)],
    )
    sums = [out[0]]
    for (sx, sd), part in zip(steps[1:], out[1:]):
        sums.append(send(part, lambda row, col, dep, sx=sx, sd=sd: (row ^ 2 * sx, col, dep ^ sd)))

    done = call(
        functools.partial(finish, sizes), "finish", [], [shape((2, irreps, mb, h), BF16)] * half, limits, *sums
    )
    def home(row, col, dep):
        return (row ^ 1, col ^ half, dep) if row % 2 else (row ^ 1, col, dep)

    back = [send(done[q], chunk(q) if q else home) for q in range(half)]
    give = call(functools.partial(settle, half), "settle", [], shape((half, irreps, mb, h), BF16), *back[::-1])
    whole = shape((cols, irreps, mb, h), BF16)
    scratch = [pltpu.VMEM((irreps, mb, h), BF16), pltpu.SemaphoreType.DMA((half,))]
    placed = call(functools.partial(place, half), "place", [], whole, done[0], *back[::-1], scratch=scratch, to=HBM)
    result = call(
        functools.partial(complete, half), "complete", [], whole, back[0], send(give, other_core), placed,
        scratch=scratch, to=HBM, last=[HBM], aliases={2: 0},
    )
    return result.transpose(0, 3, 1, 2)


def solution(mesh):
    sizes = tuple(mesh.shape[a] for a in AXES)
    in_specs = (P(None, "col", ("row", "depth")), P(None, ("row", "depth"), "col"), P(), P())
    out_specs = P(None, ("row", "depth"), None, "col")
    return jax.shard_map(
        functools.partial(body, sizes), mesh=mesh, in_specs=in_specs, out_specs=out_specs, check_vma=False
    )
```

```python
import functools

import jax
import jax.numpy as jnp
from jax import lax
from jax.experimental import pallas as pl
from jax.experimental.pallas import tpu as pltpu
from jax.sharding import PartitionSpec as P

F32 = jnp.float32
BF16 = jnp.bfloat16
AXES = ("row", "col", "depth")
VMEM = pl.BlockSpec(memory_space=pltpu.VMEM)
HBM = pl.BlockSpec(memory_space=pltpu.HBM)


def load(occ, live, ints, held, limits, counts, sem):
    irreps = ints.shape[0]
    copies = [(occ, counts.at[0]), (live, counts.at[1])] + [(ints.at[g], held.at[g]) for g in range(irreps)]
    copies = [pltpu.make_async_copy(src, dst, sem.at[i]) for i, (src, dst) in enumerate(copies)]
    for one in reversed(copies):
        one.start()
    for one in copies:
        one.wait()
    for kind in range(2):
        for g in range(irreps):
            limits[kind, g] = jnp.full(limits.shape[2:], counts[kind, g], jnp.int32)


def fetch(src, dst, sem):
    one = pltpu.make_async_copy(src, dst, sem)
    one.start()
    one.wait()


def join(mine, other, both):
    both[0] = mine[...]
    both[1] = other[...]


def products(sizes, steps, *refs):
    rows, cols, depths = sizes
    half = cols // 2
    limits, mine = refs[:2]
    came = refs[2 : 2 + half]
    ints, ints_other = refs[2 + half : 4 + half]
    outs = refs[4 + half : -1]
    turned = refs[-1]
    row, col, dep = (lax.axis_index(a) for a in AXES)
    core = lax.rem(row, 2)
    _, irreps, mb, kb = mine.shape
    row_of = (row, row ^ 1)
    totals = []
    for g in range(irreps):
        total = None
        for part in range(2):
            kstart = (row_of[part] * depths + dep) * kb
            live = limits[1, g][:1, :1]
            k_live = kstart + lax.broadcasted_iota(jnp.int32, (mb, kb), 1) < live
            lhs = []
            for q in range(half):
                m = (col ^ (q + core * half)) * mb + lax.broadcasted_iota(jnp.int32, (mb, kb), 0)
                amp = came[q][part, g].astype(F32)
                if q == 0:
                    amp = jnp.where(core == 0, mine[part, g].astype(F32), amp)
                lhs.append(jnp.where(k_live & (m < limits[0, g][:1, :1]), amp, 0.0))
            lhs = jnp.concatenate(lhs, axis=0).astype(BF16)
            term = jnp.dot(lhs, (ints, ints_other)[part][g], preferred_element_type=F32)
            total = term if total is None else total + term
        totals.append(total)
    turned[...] = jnp.concatenate(totals, axis=0).T
    h = outs[0].shape[0] // 2
    for (near, far), out in zip(steps, outs):
        sx, sd = (jnp.where(core == 0, a, b) for a, b in zip(near, far))
        for c in range(2):
            block = ((row // 2 ^ sx) * 2 + c) * depths + (dep ^ sd)
            out[c * h : (c + 1) * h] = turned[pl.ds(pl.multiple_of(block * h, 8), h), :]


def finish(sizes, *refs):
    rows, cols, depths = sizes
    half = cols // 2
    limits = refs[0]
    outs = refs[-half:]
    ins = refs[1:-half]
    row, col, dep = (lax.axis_index(a) for a in AXES)
    core = lax.rem(row, 2)
    _, irreps, mb, h = outs[0].shape
    total = ins[0][...]
    for ref in ins[1:]:
        total = total + ref[...]
    lanes = total.shape[1]
    for c in range(2):
        part = total[c * h : (c + 1) * h]
        if h % 128:
            part = jnp.concatenate([part, jnp.zeros((-h % 128, lanes), F32)], axis=0)
        part = part.T[:, :h]
        slot = ((col * rows + row - core + c) * depths + dep) * h + lax.broadcasted_iota(jnp.int32, (mb, h), 1)
        for g in range(irreps):
            for q in range(half):
                at = (g * half + q) * mb
                outs[q][c, g] = jnp.where(slot < limits[1, g][:1, :1], part[at : at + mb], 0.0).astype(BF16)


def settle(half, *refs):
    back, give = refs[:half][::-1], refs[-1]
    core = lax.rem(lax.axis_index("row"), 2)
    for q in range(half):
        give[q] = back[q][1 - core]


def assemble(half, first, *refs):
    back, came, out = refs[:half][::-1], refs[-2], refs[-1]
    core = lax.rem(lax.axis_index("row"), 2)
    col = lax.axis_index("col")

    def pick(zero, one):
        return jnp.where(core == 0, zero.astype(F32), one.astype(F32)).astype(BF16)

    out[col] = pick(first[0], back[0][1])
    out[col ^ half] = pick(back[0][0], came[0])
    for q in range(1, half):
        out[col ^ (q + core * half)] = back[q][core]
        out[col ^ (q + (1 - core) * half)] = came[q]


def call(kernel, name, specs, outs, *args, scratch=()):
    many = isinstance(outs, list)
    return pl.pallas_call(
        kernel,
        name=name,
        out_shape=outs,
        in_specs=specs + [VMEM] * (len(args) - len(specs)),
        out_specs=[VMEM] * len(outs) if many else VMEM,
        scratch_shapes=list(scratch),
        compiler_params=pltpu.CompilerParams(vmem_limit_bytes=40 * 2**20),
    )(*args)


def body(sizes, amplitudes, integrals, occ_count, virtual_pair_count):
    rows, cols, depths = sizes
    chips, half = rows // 2, cols // 2
    irreps, mb, kb = amplitudes.shape
    nb = integrals.shape[2]
    h = nb // (rows * depths)
    shape = jax.ShapeDtypeStruct

    def pairs(move):
        out = []
        for row in range(rows):
            for col in range(cols):
                for dep in range(depths):
                    r, c, d = move(row, col, dep)
                    out.append(((row * cols + col) * depths + dep, (r * cols + c) * depths + d))
        return out

    def send(value, move):
        return lax.ppermute(value, AXES, pairs(move))

    def other_core(row, col, dep):
        return row ^ 1, col, dep

    def chunk(q):
        def move(row, col, dep):
            if row % 2:
                return row, col ^ (q + half), dep
            return (row, col ^ q, dep) if q else (row ^ 2, col, dep)

        return move

    amps_other = send(amplitudes, other_core)
    held = (occ_count, virtual_pair_count, integrals)
    held = [pltpu.with_memory_space_constraint(x, pltpu.HBM) for x in held]
    ints, limits = call(
        load, "load", [HBM] * 3, [shape(integrals.shape, BF16), shape((2, irreps, 8, 128), jnp.int32)], *held,
        scratch=[pltpu.SMEM((2, irreps), jnp.int32), pltpu.SemaphoreType.DMA((2 + irreps,))],
    )
    mine = call(
        fetch, "fetch", [HBM], shape(amplitudes.shape, BF16), pltpu.with_memory_space_constraint(amplitudes, pltpu.HBM),
        scratch=[pltpu.SemaphoreType.DMA],
    )
    both = call(join, "join", [], shape((2, irreps, mb, kb), BF16), mine, amps_other)
    later, both = lax.optimization_barrier((integrals, both))
    ints_other = send(later, other_core)
    came = [send(both, chunk(q)) for q in range(half)]

    steps = [(sx, sd) for sx in range(chips) for sd in range(depths)]
    others = steps[1:-1]
    steps = [(steps[0],) * 2, (steps[-1],) * 2] + list(zip(others, others[::-1]))
    lanes = irreps * half * mb
    out = call(
        functools.partial(products, sizes, steps), "products", [], [shape((2 * h, lanes), F32)] * len(steps),
        limits, both, *came, ints, ints_other,
        scratch=[pltpu.VMEM((nb, lanes), F32)],
    )
    sums = [out[0]]
    for pair, part in zip(steps[1:], out[1:]):

        def across(row, col, dep, pair=pair):
            sx, sd = pair[row % 2]
            return row ^ 2 * sx, col, dep ^ sd

        sums.append(send(part, across))

    done = call(
        functools.partial(finish, sizes), "finish", [], [shape((2, irreps, mb, h), BF16)] * half, limits, *sums
    )
    def home(row, col, dep):
        return (row ^ 1, col ^ half, dep) if row % 2 else (row ^ 1, col, dep)

    back = [send(done[q], chunk(q) if q else home) for q in range(half)]
    give = call(functools.partial(settle, half), "settle", [], shape((half, irreps, mb, h), BF16), *back[::-1])
    result = call(
        functools.partial(assemble, half), "assemble", [], shape((cols, irreps, mb, h), BF16),
        done[0], *back[::-1], send(give, other_core),
    )
    return result.transpose(0, 3, 1, 2)


def solution(mesh):
    sizes = tuple(mesh.shape[a] for a in AXES)
    in_specs = (P(None, "col", ("row", "depth")), P(None, ("row", "depth"), "col"), P(), P())
    out_specs = P(None, ("row", "depth"), None, "col")
    return jax.shard_map(
        functools.partial(body, sizes), mesh=mesh, in_specs=in_specs, out_specs=out_specs, check_vma=False
    )
```

```python
import functools

import jax
import jax.numpy as jnp
from jax import lax
from jax.experimental import pallas as pl
from jax.experimental.pallas import tpu as pltpu
from jax.sharding import PartitionSpec as P

F32 = jnp.float32
BF16 = jnp.bfloat16
AXES = ("row", "col", "depth")
VMEM = pl.BlockSpec(memory_space=pltpu.VMEM)
HBM = pl.BlockSpec(memory_space=pltpu.HBM)


def load(occ, live, ints, held, limits, counts, sem):
    irreps = ints.shape[0]
    copies = [(occ, counts.at[0]), (live, counts.at[1])] + [(ints.at[g], held.at[g]) for g in range(irreps)]
    copies = [pltpu.make_async_copy(src, dst, sem.at[i]) for i, (src, dst) in enumerate(copies)]
    for one in reversed(copies):
        one.start()
    for one in copies:
        one.wait()
    for kind in range(2):
        for g in range(irreps):
            limits[kind, g] = jnp.full(limits.shape[2:], counts[kind, g], jnp.int32)


def copy(src, dst):
    dst[...] = src[...]


def join(mine, other, both):
    both[0] = mine[...]
    both[1] = other[...]


def products(sizes, steps, *refs):
    rows, cols, depths = sizes
    half = cols // 2
    limits, mine = refs[:2]
    came = refs[2 : 2 + half]
    ints, ints_other = refs[2 + half : 4 + half]
    outs = refs[4 + half : -1]
    turned = refs[-1]
    row, col, dep = (lax.axis_index(a) for a in AXES)
    core = lax.rem(row, 2)
    _, irreps, mb, kb = mine.shape
    row_of = (row, row ^ 1)
    totals = []
    for g in range(irreps):
        total = None
        for part in range(2):
            kstart = (row_of[part] * depths + dep) * kb
            live = limits[1, g][:1, :1]
            k_live = kstart + lax.broadcasted_iota(jnp.int32, (mb, kb), 1) < live
            lhs = []
            for q in range(half):
                m = (col ^ (q + core * half)) * mb + lax.broadcasted_iota(jnp.int32, (mb, kb), 0)
                amp = came[q][part, g].astype(F32)
                if q == 0:
                    amp = jnp.where(core == 0, mine[part, g].astype(F32), amp)
                lhs.append(jnp.where(k_live & (m < limits[0, g][:1, :1]), amp, 0.0))
            lhs = jnp.concatenate(lhs, axis=0).astype(BF16)
            term = jnp.dot(lhs, (ints, ints_other)[part][g], preferred_element_type=F32)
            total = term if total is None else total + term
        totals.append(total)
    turned[...] = jnp.concatenate(totals, axis=0).T
    h = outs[0].shape[0] // 2
    for (sx, sd), out in zip(steps, outs):
        for c in range(2):
            block = ((row // 2 ^ sx) * 2 + c) * depths + (dep ^ sd)
            out[c * h : (c + 1) * h] = turned[pl.ds(pl.multiple_of(block * h, 8), h), :]


def finish(sizes, *refs):
    rows, cols, depths = sizes
    half = cols // 2
    limits = refs[0]
    outs = refs[-half:]
    ins = refs[1:-half]
    row, col, dep = (lax.axis_index(a) for a in AXES)
    core = lax.rem(row, 2)
    _, irreps, mb, h = outs[0].shape
    total = ins[0][...]
    for ref in ins[1:]:
        total = total + ref[...]
    lanes = total.shape[1]
    for c in range(2):
        part = total[c * h : (c + 1) * h]
        if h % 128:
            part = jnp.concatenate([part, jnp.zeros((-h % 128, lanes), F32)], axis=0)
        part = part.T[:, :h]
        slot = ((col * rows + row - core + c) * depths + dep) * h + lax.broadcasted_iota(jnp.int32, (mb, h), 1)
        for g in range(irreps):
            for q in range(half):
                at = (g * half + q) * mb
                outs[q][c, g] = jnp.where(slot < limits[1, g][:1, :1], part[at : at + mb], 0.0).astype(BF16)


def settle(half, *refs):
    back, give = refs[:half][::-1], refs[-1]
    core = lax.rem(lax.axis_index("row"), 2)
    for q in range(half):
        give[q] = back[q][1 - core]


def assemble(half, first, *refs):
    back, came, out = refs[:half][::-1], refs[-2], refs[-1]
    core = lax.rem(lax.axis_index("row"), 2)
    col = lax.axis_index("col")

    def pick(zero, one):
        return jnp.where(core == 0, zero.astype(F32), one.astype(F32)).astype(BF16)

    out[col] = pick(first[0], back[0][1])
    out[col ^ half] = pick(back[0][0], came[0])
    for q in range(1, half):
        out[col ^ (q + core * half)] = back[q][core]
        out[col ^ (q + (1 - core) * half)] = came[q]


def call(kernel, name, specs, outs, *args, scratch=()):
    many = isinstance(outs, list)
    return pl.pallas_call(
        kernel,
        name=name,
        out_shape=outs,
        in_specs=specs + [VMEM] * (len(args) - len(specs)),
        out_specs=[VMEM] * len(outs) if many else VMEM,
        scratch_shapes=list(scratch),
        compiler_params=pltpu.CompilerParams(vmem_limit_bytes=40 * 2**20),
    )(*args)


def body(sizes, amplitudes, integrals, occ_count, virtual_pair_count):
    rows, cols, depths = sizes
    chips, half = rows // 2, cols // 2
    irreps, mb, kb = amplitudes.shape
    nb = integrals.shape[2]
    h = nb // (rows * depths)
    shape = jax.ShapeDtypeStruct

    def pairs(move):
        out = []
        for row in range(rows):
            for col in range(cols):
                for dep in range(depths):
                    r, c, d = move(row, col, dep)
                    out.append(((row * cols + col) * depths + dep, (r * cols + c) * depths + d))
        return out

    def send(value, move):
        return lax.ppermute(value, AXES, pairs(move))

    def other_core(row, col, dep):
        return row ^ 1, col, dep

    def chunk(q):
        def move(row, col, dep):
            if row % 2:
                return row, col ^ (q + half), dep
            return (row, col ^ q, dep) if q else (row, col, dep ^ 1)

        return move

    amps_other = send(amplitudes, other_core)
    held = (occ_count, virtual_pair_count, integrals)
    held = [pltpu.with_memory_space_constraint(x, pltpu.HBM) for x in held]
    ints, limits = call(
        load, "load", [HBM] * 3, [shape(integrals.shape, BF16), shape((2, irreps, 8, 128), jnp.int32)], *held,
        scratch=[pltpu.SMEM((2, irreps), jnp.int32), pltpu.SemaphoreType.DMA((2 + irreps,))],
    )
    mine = call(copy, "fetch", [], shape(amplitudes.shape, BF16), amplitudes)
    both = call(join, "join", [], shape((2, irreps, mb, kb), BF16), mine, amps_other)
    later, both = lax.optimization_barrier((integrals, both))
    ints_other = send(later, other_core)
    came = [send(both, chunk(q)) for q in range(half)]

    steps = [(sx, sd) for sx in range(chips) for sd in range(depths)]
    steps = steps[:1] + steps[-1:] + steps[1:-1]
    lanes = irreps * half * mb
    out = call(
        functools.partial(products, sizes, steps), "products", [], [shape((2 * h, lanes), F32)] * len(steps),
        limits, both, *came, ints, ints_other,
        scratch=[pltpu.VMEM((nb, lanes), F32)],
    )
    sums = [out[0]]
    for (sx, sd), part in zip(steps[1:], out[1:]):
        sums.append(send(part, lambda row, col, dep, sx=sx, sd=sd: (row ^ 2 * sx, col, dep ^ sd)))

    done = call(
        functools.partial(finish, sizes), "finish", [], [shape((2, irreps, mb, h), BF16)] * half, limits, *sums
    )
    def home(row, col, dep):
        return (row ^ 1, col ^ half, dep) if row % 2 else (row ^ 1, col, dep)

    back = [send(done[q], chunk(q) if q else home) for q in range(half)]
    give = call(functools.partial(settle, half), "settle", [], shape((half, irreps, mb, h), BF16), *back[::-1])
    result = call(
        functools.partial(assemble, half), "assemble", [], shape((cols, irreps, mb, h), BF16),
        done[0], *back[::-1], send(give, other_core),
    )
    return result.transpose(0, 3, 1, 2)


def solution(mesh):
    sizes = tuple(mesh.shape[a] for a in AXES)
    in_specs = (P(None, "col", ("row", "depth")), P(None, ("row", "depth"), "col"), P(), P())
    out_specs = P(None, ("row", "depth"), None, "col")
    return jax.shard_map(
        functools.partial(body, sizes), mesh=mesh, in_specs=in_specs, out_specs=out_specs, check_vma=False
    )
```

```python
import functools

import jax
import jax.numpy as jnp
from jax import lax
from jax.experimental import pallas as pl
from jax.experimental.pallas import tpu as pltpu
from jax.sharding import PartitionSpec as P

F32 = jnp.float32
BF16 = jnp.bfloat16
AXES = ("row", "col", "depth")
VMEM = pl.BlockSpec(memory_space=pltpu.VMEM)
HBM = pl.BlockSpec(memory_space=pltpu.HBM)


def load(occ, live, ints, held, limits, counts, sem):
    irreps = ints.shape[0]
    copies = [(occ, counts.at[0]), (live, counts.at[1])] + [(ints.at[g], held.at[g]) for g in range(irreps)]
    copies = [pltpu.make_async_copy(src, dst, sem.at[i]) for i, (src, dst) in enumerate(copies)]
    for one in reversed(copies):
        one.start()
    for one in copies:
        one.wait()
    for kind in range(2):
        for g in range(irreps):
            limits[kind, g] = jnp.full(limits.shape[2:], counts[kind, g], jnp.int32)


def fetch(src, dst, sem):
    one = pltpu.make_async_copy(src, dst, sem)
    one.start()
    one.wait()


def join(mine, other, both):
    both[0] = mine[...]
    both[1] = other[...]


def products(sizes, steps, *refs):
    rows, cols, depths = sizes
    half = cols // 2
    limits, mine = refs[:2]
    came = refs[2 : 2 + half]
    ints, ints_other = refs[2 + half : 4 + half]
    outs = refs[4 + half : -1]
    turned = refs[-1]
    row, col, dep = (lax.axis_index(a) for a in AXES)
    core = lax.rem(row, 2)
    _, irreps, mb, kb = mine.shape
    row_of = (row, row ^ 1)
    totals = []
    for g in range(irreps):
        total = None
        for part in range(2):
            kstart = (row_of[part] * depths + dep) * kb
            live = limits[1, g][:1, :1]
            k_live = kstart + lax.broadcasted_iota(jnp.int32, (mb, kb), 1) < live
            lhs = []
            for q in range(half):
                m = (col ^ (q + core * half)) * mb + lax.broadcasted_iota(jnp.int32, (mb, kb), 0)
                amp = came[q][part, g].astype(F32)
                if q == 0:
                    amp = jnp.where(core == 0, mine[part, g].astype(F32), amp)
                lhs.append(jnp.where(k_live & (m < limits[0, g][:1, :1]), amp, 0.0))
            lhs = jnp.concatenate(lhs, axis=0).astype(BF16)
            term = jnp.dot(lhs, (ints, ints_other)[part][g], preferred_element_type=F32)
            total = term if total is None else total + term
        totals.append(total)
    turned[...] = jnp.concatenate(totals, axis=0).T
    h = outs[0].shape[0] // 2
    for (sx, sd), out in zip(steps, outs):
        for c in range(2):
            block = ((row // 2 ^ sx) * 2 + c) * depths + (dep ^ sd)
            out[c * h : (c + 1) * h] = turned[pl.ds(pl.multiple_of(block * h, 8), h), :]


def finish(sizes, *refs):
    rows, cols, depths = sizes
    half = cols // 2
    limits = refs[0]
    outs = refs[-half:]
    ins = refs[1:-half]
    row, col, dep = (lax.axis_index(a) for a in AXES)
    core = lax.rem(row, 2)
    _, irreps, mb, h = outs[0].shape
    total = ins[0][...]
    for ref in ins[1:]:
        total = total + ref[...]
    lanes = total.shape[1]
    for c in range(2):
        part = total[c * h : (c + 1) * h]
        if h % 128:
            part = jnp.concatenate([part, jnp.zeros((-h % 128, lanes), F32)], axis=0)
        part = part.T[:, :h]
        slot = ((col * rows + row - core + c) * depths + dep) * h + lax.broadcasted_iota(jnp.int32, (mb, h), 1)
        for g in range(irreps):
            for q in range(half):
                at = (g * half + q) * mb
                outs[q][c, g] = jnp.where(slot < limits[1, g][:1, :1], part[at : at + mb], 0.0).astype(BF16)


def settle(half, *refs):
    back, give = refs[:half][::-1], refs[-1]
    core = lax.rem(lax.axis_index("row"), 2)
    for q in range(half):
        give[q] = back[q][1 - core]


def assemble(half, first, *refs):
    back, came, out = refs[:half][::-1], refs[-2], refs[-1]
    core = lax.rem(lax.axis_index("row"), 2)
    col = lax.axis_index("col")

    def pick(zero, one):
        return jnp.where(core == 0, zero.astype(F32), one.astype(F32)).astype(BF16)

    out[col] = pick(first[0], back[0][1])
    out[col ^ half] = pick(back[0][0], came[0])
    for q in range(1, half):
        out[col ^ (q + core * half)] = back[q][core]
        out[col ^ (q + (1 - core) * half)] = came[q]


def call(kernel, name, specs, outs, *args, scratch=()):
    many = isinstance(outs, list)
    return pl.pallas_call(
        kernel,
        name=name,
        out_shape=outs,
        in_specs=specs + [VMEM] * (len(args) - len(specs)),
        out_specs=[VMEM] * len(outs) if many else VMEM,
        scratch_shapes=list(scratch),
        compiler_params=pltpu.CompilerParams(vmem_limit_bytes=40 * 2**20),
    )(*args)


def body(sizes, amplitudes, integrals, occ_count, virtual_pair_count):
    rows, cols, depths = sizes
    chips, half = rows // 2, cols // 2
    irreps, mb, kb = amplitudes.shape
    nb = integrals.shape[2]
    h = nb // (rows * depths)
    shape = jax.ShapeDtypeStruct

    def pairs(move):
        out = []
        for row in range(rows):
            for col in range(cols):
                for dep in range(depths):
                    r, c, d = move(row, col, dep)
                    out.append(((row * cols + col) * depths + dep, (r * cols + c) * depths + d))
        return out

    def send(value, move):
        return lax.ppermute(value, AXES, pairs(move))

    def other_core(row, col, dep):
        return row ^ 1, col, dep

    def chunk(q):
        def move(row, col, dep):
            if row % 2:
                return row, col ^ (q + half), dep
            return (row, col ^ q, dep) if q else (row ^ 2, col, dep)

        return move

    amps_other = send(amplitudes, other_core)
    held = (occ_count, virtual_pair_count, integrals)
    held = [pltpu.with_memory_space_constraint(x, pltpu.HBM) for x in held]
    ints, limits = call(
        load, "load", [HBM] * 3, [shape(integrals.shape, BF16), shape((2, irreps, 8, 128), jnp.int32)], *held,
        scratch=[pltpu.SMEM((2, irreps), jnp.int32), pltpu.SemaphoreType.DMA((2 + irreps,))],
    )
    mine = call(
        fetch, "fetch", [HBM], shape(amplitudes.shape, BF16), pltpu.with_memory_space_constraint(amplitudes, pltpu.HBM),
        scratch=[pltpu.SemaphoreType.DMA],
    )
    both = call(join, "join", [], shape((2, irreps, mb, kb), BF16), mine, amps_other)
    later, both = lax.optimization_barrier((integrals, both))
    ints_other = send(later, other_core)
    came = [send(both, chunk(q)) for q in range(half)]

    steps = [(sx, sd) for sx in range(chips) for sd in range(depths)]
    steps = steps[:1] + steps[:0:-1]
    lanes = irreps * half * mb
    out = call(
        functools.partial(products, sizes, steps), "products", [], [shape((2 * h, lanes), F32)] * len(steps),
        limits, both, *came, ints, ints_other,
        scratch=[pltpu.VMEM((nb, lanes), F32)],
    )
    sums = [out[0]]
    for (sx, sd), part in zip(steps[1:], out[1:]):
        sums.append(send(part, lambda row, col, dep, sx=sx, sd=sd: (row ^ 2 * sx, col, dep ^ sd)))

    done = call(
        functools.partial(finish, sizes), "finish", [], [shape((2, irreps, mb, h), BF16)] * half, limits, *sums
    )
    def home(row, col, dep):
        return (row ^ 1, col ^ half, dep) if row % 2 else (row ^ 1, col, dep)

    back = [send(done[q], chunk(q) if q else home) for q in range(half)]
    give = call(functools.partial(settle, half), "settle", [], shape((half, irreps, mb, h), BF16), *back[::-1])
    result = call(
        functools.partial(assemble, half), "assemble", [], shape((cols, irreps, mb, h), BF16),
        done[0], *back[::-1], send(give, other_core),
    )
    return result.transpose(0, 3, 1, 2)


def solution(mesh):
    sizes = tuple(mesh.shape[a] for a in AXES)
    in_specs = (P(None, "col", ("row", "depth")), P(None, ("row", "depth"), "col"), P(), P())
    out_specs = P(None, ("row", "depth"), None, "col")
    return jax.shard_map(
        functools.partial(body, sizes), mesh=mesh, in_specs=in_specs, out_specs=out_specs, check_vma=False
    )
```
